32 devices in a mesh: dp: 8 (over z, y), mp: 4 (over x, core).
Axes of the slice: x: 2, y: 2, z: 4, core: 2. Of those that a mesh axis runs over, the one named last changes fastest.
Arguments:
- token_ids: int32 [64, 512], P('dp'), may hold values from 0 to 30719
- segment_ids: int32 [64, 512], P('dp'), may hold values from 0 to 1, as said below
- task_ids: int32 [64], P('dp'), may hold values from 0 to 3, as said below
- task_order: int32 [4], replicated, may hold values from 0 to 3, each once
- counted: int32 [64, 512], P('dp'), may hold values from 0 to 1, as said below
- targets: float32 [64, 512], P('dp'), may hold values from -6 to 6
- word_table: float32 [15360, 1536], P('dp', 'mp'), may hold values from -0.24 to 0.24
- word_first: float32 [15360, 1536], P('dp', 'mp'), may hold values from -5.722046e-06 to 5.722046e-06
- word_second: float32 [15360, 1536], P('dp', 'mp'), may hold values from 8.043907e-14 to 3.217563e-13
- tables: float32 [514, 768], P(None, 'dp'), may hold values from -0.24 to 0.24
- tables_first: float32 [514, 768], P(None, 'dp'), may hold values from -5.722046e-06 to 5.722046e-06
- tables_second: float32 [514, 768], P(None, 'dp'), may hold values from 8.043907e-14 to 3.217563e-13
- matrices: float32 [768, 9216], P('dp', 'mp')
- matrices_first: float32 [768, 9216], P('dp', 'mp'), may hold values from -5.722046e-06 to 5.722046e-06
- matrices_second: float32 [768, 9216], P('dp', 'mp'), may hold values from 8.043907e-14 to 3.217563e-13
- vectors: float32 [14, 768], P(None, 'dp')
- vectors_first: float32 [14, 768], P(None, 'dp'), may hold values from -5.722046e-06 to 5.722046e-06
- vectors_second: float32 [14, 768], P(None, 'dp'), may hold values from 8.043907e-14 to 3.217563e-13
- regressor: float32 [4, 768], P(None, 'dp'), may hold values from -0.21875 to 0.21875
- regressor_first: float32 [4, 768], P(None, 'dp'), may hold values from -5.722046e-06 to 5.722046e-06
- regressor_second: float32 [4, 768], P(None, 'dp'), may hold values from 8.043907e-14 to 3.217563e-13
Outputs:
- word_grad: float32 [15360, 1536], P('dp', 'mp')
- word_moment: float32 [15360, 1536], P('dp', 'mp')
- word_square: float32 [15360, 1536], P('dp', 'mp')
- word_weight: float32 [15360, 1536], P('dp', 'mp')
- tables_grad: float32 [514, 768], P(None, 'dp')
- tables_moment: float32 [514, 768], P(None, 'dp')
- tables_square: float32 [514, 768], P(None, 'dp')
- tables_weight: float32 [514, 768], P(None, 'dp')
- matrices_grad: float32 [768, 9216], P('dp', 'mp')
- matrices_moment: float32 [768, 9216], P('dp', 'mp')
- matrices_square: float32 [768, 9216], P('dp', 'mp')
- matrices_weight: float32 [768, 9216], P('dp', 'mp')
- vectors_grad: float32 [14, 768], P(None, 'dp')
- vectors_moment: float32 [14, 768], P(None, 'dp')
- vectors_square: float32 [14, 768], P(None, 'dp')
- vectors_weight: float32 [14, 768], P(None, 'dp')
- regressor_grad: float32 [4, 768], P(None, 'dp')
- regressor_moment: float32 [4, 768], P(None, 'dp')
- regressor_square: float32 [4, 768], P(None, 'dp')
- regressor_weight: float32 [4, 768], P(None, 'dp')
- grad_norm: float32 [], replicated
- loss_total: float32 [], replicated
- task_counts: float32 [4], replicated
The draws below stay inside these ranges and needn't reach their ends.
Inputs may be any that keep to these rules, and one draw needn't show every extreme that they name: `segment_ids`: each row holds zeros and then ones, both present; the first one stands between positions 128 and 384. `task_ids`: every task occurs in some example. `task_order`: A permutation of the 4 tasks. `counted`: position 0 of every example counts.
All inputs are finite; a program needn't handle non-finite values.
Results may differ from the reference program's by a relative error of at most 0.0035.
The reference program's roundings to bfloat16 on the way count: a program that leaves them out, or rounds other values in their place, can miss the bound.
Values may be sent and summed in bfloat16 or wider, within the bound.
No kernel may reach another device: no remote copies, remote signals or barrier semaphores. Data moves between devices by JAX's collectives and lax.ppermute only.
A program may use at most 384 MiB of HBM per device.

```python
import math
import jax
import jax.numpy as jnp
import numpy as np
from jax import lax

D = 768
HEADS = 12
HEAD = 64
FF = 3072
VOCAB = 30720
SEQ = 512
TASKS = 4
VECTORS = 14
STEP = 5
EXAMPLES = 64
UNITS_OWN = 192
N_MP = 4


def draw_segment_ids(key, part):
    key = jax.random.fold_in(key, 4)
    boundary = jax.random.randint(key, (EXAMPLES, 1), SEQ // 4, 3 * SEQ // 4 + 1)
    return (jnp.arange(SEQ)[None, :] >= boundary).astype(jnp.int32)


def draw_task_ids(key, part):
    key = jax.random.fold_in(key, 2)
    first_key, second_key = jax.random.split(key)
    picks = jax.random.randint(first_key, (EXAMPLES,), 0, 10)
    chosen = (picks >= 4).astype(jnp.int32) + (picks >= 7).astype(jnp.int32) + (picks >= 9).astype(jnp.int32)
    chosen = jnp.minimum(chosen, TASKS - 1)
    order = jax.random.permutation(second_key, TASKS).astype(jnp.int32)
    return chosen.at[:TASKS].set(order)


def draw_counted(key, part):
    key = jax.random.fold_in(key, 3)
    example_rows = jnp.arange(EXAMPLES, dtype=jnp.int32)[:, None]
    limit = 250 + 500 * example_rows // max(EXAMPLES - 1, 1)
    picks = jax.random.randint(key, (EXAMPLES, SEQ), 0, 1000)
    marked = (picks < limit).astype(jnp.int32)
    return marked.at[:, 0].set(1)


def draw_matrices(key, part):
    key = jax.random.fold_in(key, 5)
    block_index = (jnp.arange(12 * D) % (12 * UNITS_OWN) // UNITS_OWN)[None, :]
    factor = jnp.where(block_index < 3, D ** (-0.5), jnp.where(block_index == 3, 0.5 * (SEQ / D) ** 0.5, jnp.where(block_index < 8, D ** (-0.5), FF ** (-0.5))))
    entries = jax.random.normal(key, (D, 12 * D), jnp.float32)
    return entries * factor


def draw_vectors(key, part):
    key = jax.random.fold_in(key, 6)
    first_key, second_key = jax.random.split(key)
    column = jnp.arange(D, dtype=jnp.float32)[None, :] / (D - 1)
    row_index = jnp.arange(VECTORS)[:, None]
    noise = jax.random.uniform(first_key, (VECTORS, D), jnp.float32, 0.85, 1.15)
    rising = 0.6 + 1.2 * column
    biases = 0.3 * jax.random.normal(second_key, (VECTORS, D), jnp.float32)
    is_gain = (row_index == 0) | (row_index == 5) | (row_index == 12)
    return jnp.where(is_gain, rising * noise, biases)


def with_ends(values, rng, low, largest):
    longest = values.shape.index(max(values.shape))
    spots = []
    for shift in (0, 1):
        where = [jax.random.randint(jax.random.fold_in(rng, axis), (), 0, length) for axis, length in enumerate(values.shape)]
        where[longest] = (where[longest] + shift) % values.shape[longest]
        spots.append(tuple(where))
    return values.at[spots[0]].set(low).at[spots[1]].set(largest)


def levels(rng, dims, shards, least, high):
    loudness = 1.0
    for dim, blocks in shards:
        draws = jax.random.uniform(jax.random.fold_in(jax.random.fold_in(rng, 6), dim), (blocks,), jnp.float32, least / len(shards), high / len(shards))
        loudness = loudness * jnp.repeat(jnp.exp(draws), dims[dim] // blocks).reshape((-1,) + (1,) * (len(dims) - 1 - dim))
    return loudness


def rank_table(number_of, slope):
    weights = [(1 << 20) // math.isqrt(grade ** slope) + 1 for grade in range(1, number_of + 1)]
    width = 1 + sum(weights) // (1 << 30)
    return np.cumsum(np.array([max(1, weight // width) for weight in weights]))


def ranked_ids(rng, extent, number_of, skew):
    grid = rank_table(number_of, skew)
    pick = jax.random.randint(jax.random.fold_in(rng, 1), extent, 0, int(grid[number_of - 1]))
    grade = jnp.searchsorted(jnp.asarray(grid, jnp.int32), pick, side="right")
    return jax.random.permutation(jax.random.fold_in(rng, 2), number_of)[grade].astype(jnp.int32)


def gaussian(stream_key, extent, scale, most, cuts=(), kind=jnp.bfloat16):
    level = levels(stream_key, extent, cuts, -0.22, 0.18) if cuts else 1.0
    result = jax.random.normal(stream_key, extent, jnp.float32) * scale * level
    return jnp.minimum(jnp.maximum(result, -most), most).astype(kind)


def setup_inputs(seed: int = 0) -> dict:
    keys = jax.random.split(jax.random.key(seed), 22)
    return {
        "token_ids": with_ends(ranked_ids(keys[0], (EXAMPLES, SEQ), VOCAB, 2), jax.random.fold_in(keys[0], 3), 0, VOCAB - 1).astype(jnp.int32),
        "segment_ids": draw_segment_ids(jax.random.fold_in(keys[21], 71), 0),
        "task_ids": draw_task_ids(jax.random.fold_in(keys[21], 71), 0),
        "task_order": jax.random.permutation(keys[3], TASKS).astype(jnp.int32),
        "counted": draw_counted(jax.random.fold_in(keys[21], 71), 0),
        "targets": gaussian(keys[5], (EXAMPLES, SEQ), 1.0, 6.0, ((0, 8),), jnp.float32),
        "word_table": gaussian(keys[6], (VOCAB // 2, 2 * D), 0.04, 0.24, ((0, 8), (1, 4)), jnp.float32),
        "word_first": gaussian(keys[7], (VOCAB // 2, 2 * D), (0.0055 / (VOCAB * D + (SEQ + 2) * D + 12 * D * D + VECTORS * D + TASKS * D) ** 0.5), 5.7220458984375e-06, ((0, 8), (1, 4)), jnp.float32),
        "word_second": jnp.clip(8.043907337093592e-14 + 2.4131722011280776e-13 * jax.random.uniform(keys[8], (VOCAB // 2, 2 * D), jnp.float32) ** levels(keys[8], (VOCAB // 2, 2 * D), ((0, 8), (1, 4)), -0.2, 0.2), 8.043907337093592e-14, 3.217562934837437e-13),
        "tables": gaussian(keys[9], (SEQ + 2, D), 0.04, 0.24, ((1, 8),), jnp.float32),
        "tables_first": gaussian(keys[10], (SEQ + 2, D), (0.0055 / (VOCAB * D + (SEQ + 2) * D + 12 * D * D + VECTORS * D + TASKS * D) ** 0.5), 5.7220458984375e-06, ((1, 8),), jnp.float32),
        "tables_second": jnp.clip(8.043907337093592e-14 + 2.4131722011280776e-13 * jax.random.uniform(keys[11], (SEQ + 2, D), jnp.float32) ** levels(keys[11], (SEQ + 2, D), ((1, 8),), -0.2, 0.2), 8.043907337093592e-14, 3.217562934837437e-13),
        "matrices": draw_matrices(jax.random.fold_in(keys[21], 71), 0),
        "matrices_first": gaussian(keys[13], (D, 12 * D), (0.0055 / (VOCAB * D + (SEQ + 2) * D + 12 * D * D + VECTORS * D + TASKS * D) ** 0.5), 5.7220458984375e-06, ((0, 8), (1, 4)), jnp.float32),
        "matrices_second": jnp.clip(8.043907337093592e-14 + 2.4131722011280776e-13 * jax.random.uniform(keys[14], (D, 12 * D), jnp.float32) ** levels(keys[14], (D, 12 * D), ((0, 8), (1, 4)), -0.2, 0.2), 8.043907337093592e-14, 3.217562934837437e-13),
        "vectors": draw_vectors(jax.random.fold_in(keys[21], 71), 0),
        "vectors_first": gaussian(keys[16], (VECTORS, D), (0.0055 / (VOCAB * D + (SEQ + 2) * D + 12 * D * D + VECTORS * D + TASKS * D) ** 0.5), 5.7220458984375e-06, ((1, 8),), jnp.float32),
        "vectors_second": jnp.clip(8.043907337093592e-14 + 2.4131722011280776e-13 * jax.random.uniform(keys[17], (VECTORS, D), jnp.float32) ** levels(keys[17], (VECTORS, D), ((1, 8),), -0.2, 0.2), 8.043907337093592e-14, 3.217562934837437e-13),
        "regressor": gaussian(keys[18], (TASKS, D), D ** -0.5, 0.21875, ((1, 8),), jnp.float32),
        "regressor_first": gaussian(keys[19], (TASKS, D), (0.0055 / (VOCAB * D + (SEQ + 2) * D + 12 * D * D + VECTORS * D + TASKS * D) ** 0.5), 5.7220458984375e-06, ((1, 8),), jnp.float32),
        "regressor_second": jnp.clip(8.043907337093592e-14 + 2.4131722011280776e-13 * jax.random.uniform(keys[20], (TASKS, D), jnp.float32) ** levels(keys[20], (TASKS, D), ((1, 8),), -0.2, 0.2), 8.043907337093592e-14, 3.217562934837437e-13),
    }


@jax.custom_vjp
def low(v):
    return lax.optimization_barrier(v.astype(jnp.bfloat16)).astype(jnp.float32)

@jax.custom_vjp
def low_back(v):
    return v

def low_keep(v):
    return (low(v), None)

def low_pass(kept, grad):
    return (grad,)

def back_keep(v):
    return (v, None)

def back_low(kept, grad):
    return (low(grad),)
low.defvjp(low_keep, low_pass)
low_back.defvjp(back_keep, back_low)
HIGHEST = lax.Precision.HIGHEST
NORM_EPS = 1e-12
CLIP = 0.05
BETA_ONE = 0.9
BETA_TWO = 0.999
ADAM_EPS = 1e-08
RATE_WEIGHT = 0.03
RATE_VECTOR = 0.3
DECAY = 0.01

def word_in(stored):
    return stored.reshape(VOCAB // 2, N_MP, 2, UNITS_OWN).transpose(0, 2, 1, 3).reshape(VOCAB, D)

def word_out(plain):
    return plain.reshape(VOCAB // 2, 2, N_MP, UNITS_OWN).transpose(0, 2, 1, 3).reshape(VOCAB // 2, 2 * D)

def block_in(stored):
    return stored.reshape(D, N_MP, 12, UNITS_OWN).transpose(0, 2, 1, 3).reshape(D, 12, D)

def block_out(plain):
    return plain.reshape(D, 12, N_MP, UNITS_OWN).transpose(0, 2, 1, 3).reshape(D, 12 * D)

def layer_norm(inputs, norm_gain, norm_bias):
    center = lax.optimization_barrier(jnp.mean(inputs, axis=-1, keepdims=True))
    offset = inputs - center
    spread = lax.optimization_barrier(jnp.mean(offset * offset, axis=-1, keepdims=True))
    return offset * lax.rsqrt(spread + NORM_EPS) * norm_gain + norm_bias

def example_errors(params, token_row, segment_row, counted_row, target_row, task_row):
    word_rows, table_rows, matrix_rows, vector_rows, regressor_rows = params
    segment_part = jnp.where(segment_row[:, None] == 1, table_rows[SEQ + 1], table_rows[SEQ])
    embedded = low_back(word_rows[token_row]) + table_rows[:SEQ] + segment_part
    hidden_zero = layer_norm(embedded, vector_rows[0], vector_rows[1])
    projected = jnp.einsum('sd,dce->sce', low(hidden_zero), matrix_rows[:, 0:3, :], precision=HIGHEST)
    query_rows = low_back(low(projected[:, 0] + vector_rows[2])).reshape(SEQ, HEADS, HEAD)
    key_rows = low_back(low(projected[:, 1])).reshape(SEQ, HEADS, HEAD)
    value_rows = low_back(low(projected[:, 2] + vector_rows[3])).reshape(SEQ, HEADS, HEAD)
    scores = low_back(jnp.einsum('qhe,khe->hqk', query_rows, key_rows, precision=HIGHEST) * HEAD ** (-0.5))
    weights = low(jax.nn.softmax(scores, axis=-1))
    context = jnp.einsum('hqk,khe->qhe', weights, value_rows, precision=HIGHEST).reshape(SEQ, D)
    context = low_back(low(context))
    attended = low_back(jnp.einsum('sh,oh->so', context, matrix_rows[:, 3, :], precision=HIGHEST) + vector_rows[4])
    hidden_one = layer_norm(hidden_zero + attended, vector_rows[5], vector_rows[6])
    inner_sum = jnp.einsum('sd,dce->sce', low(hidden_one), matrix_rows[:, 4:8, :], precision=HIGHEST)
    inner_sum = low_back(inner_sum + vector_rows[7:11])
    active = low(jax.nn.gelu(inner_sum, approximate=False))
    branch_out = low_back(jnp.einsum('sce,oce->so', active, matrix_rows[:, 8:12, :], precision=HIGHEST) + vector_rows[11])
    hidden_two = layer_norm(hidden_one + branch_out, vector_rows[12], vector_rows[13])
    predicted = jnp.dot(jnp.dot(hidden_two, regressor_rows.T, precision=HIGHEST), task_row, precision=HIGHEST)
    errors = (predicted - target_row) * counted_row
    return task_row * jnp.sum(errors * errors)

def adam_update(weight, gradient, first_moment, second_moment, step_rate, weight_decay):
    moment_new = BETA_ONE * first_moment + (1.0 - BETA_ONE) * gradient
    square_new = BETA_TWO * second_moment + (1.0 - BETA_TWO) * gradient * gradient
    corrected = moment_new / (1.0 - BETA_ONE ** STEP)
    scaled = square_new / (1.0 - BETA_TWO ** STEP)
    weight_new = weight - step_rate * (corrected / (jnp.sqrt(scaled) + ADAM_EPS) + weight_decay * weight)
    return (moment_new, square_new, weight_new)

def reference(token_ids, segment_ids, task_ids, task_order, counted, targets, word_table, word_first, word_second, tables, tables_first, tables_second, matrices, matrices_first, matrices_second, vectors, vectors_first, vectors_second, regressor, regressor_first, regressor_second):
    word_table, word_first, word_second = (word_in(word_table), word_in(word_first), word_in(word_second))
    matrices, matrices_first, matrices_second = (block_in(matrices), block_in(matrices_first), block_in(matrices_second))
    task_hot = (task_ids[:, None] == jnp.arange(TASKS, dtype=jnp.int32)[None, :]).astype(jnp.float32)
    counted_float = counted.astype(jnp.float32)
    task_counts = lax.optimization_barrier(jnp.sum(task_hot * lax.optimization_barrier(jnp.sum(counted_float, axis=1))[:, None], axis=0))

    def task_losses(word_rows, table_rows, matrix_rows, vector_rows, regressor_rows):
        params = (low(word_rows), low(table_rows), low(matrix_rows), low(vector_rows), low(regressor_rows))
        step_errors = jax.checkpoint(lambda example_items: example_errors(params, *example_items))
        errors = lax.map(step_errors, (token_ids, segment_ids, counted_float, targets, task_hot))
        return lax.optimization_barrier(jnp.sum(errors, axis=0)) / task_counts
    losses, pull_back = jax.vjp(task_losses, word_table, tables, matrices, vectors, regressor)
    loss_total = jnp.sum(losses)
    identity = jnp.eye(TASKS, dtype=jnp.float32)
    per_task = [pull_back(identity[task_index]) for task_index in range(TASKS)]
    summed_grads = []
    for slot_index in range(5):
        summed = per_task[0][slot_index]
        for task_index in range(1, TASKS):
            summed = summed + per_task[task_index][slot_index]
        summed_grads.append(summed)
    flat_tasks = jnp.stack([task_grads[2] for task_grads in per_task]).reshape(TASKS, -1)
    squares = lax.optimization_barrier(jnp.sum(flat_tasks * flat_tasks, axis=1))
    surgery = jnp.zeros_like(flat_tasks[0])
    for first_task in range(TASKS):
        current = flat_tasks[first_task]
        for position in range(TASKS):
            other_task = task_order[position]
            other_grad = flat_tasks[other_task]
            inner_dot = jnp.sum(current * other_grad)
            factor = jnp.where(other_task == first_task, 0.0, jnp.minimum(inner_dot, 0.0) / squares[other_task])
            current = current - factor * other_grad
        surgery = surgery + current
    gradients = [summed_grads[0], summed_grads[1], surgery.reshape(matrices.shape), summed_grads[3], summed_grads[4]]
    squared_total = jnp.sum(gradients[0] * gradients[0])
    for gradient in gradients[1:]:
        squared_total = squared_total + jnp.sum(gradient * gradient)
    grad_norm = jnp.sqrt(squared_total)
    clip_scale = jnp.minimum(1.0, CLIP / grad_norm)
    word_grad, tables_grad, matrices_grad, vectors_grad, regressor_grad = [gradient * clip_scale for gradient in gradients]
    word_moment, word_square, word_weight = adam_update(word_table, word_grad, word_first, word_second, RATE_WEIGHT, DECAY)
    tables_moment, tables_square, tables_weight = adam_update(tables, tables_grad, tables_first, tables_second, RATE_WEIGHT, DECAY)
    matrices_moment, matrices_square, matrices_weight = adam_update(matrices, matrices_grad, matrices_first, matrices_second, RATE_WEIGHT, DECAY)
    vectors_moment, vectors_square, vectors_weight = adam_update(vectors, vectors_grad, vectors_first, vectors_second, RATE_VECTOR, 0.0)
    regressor_moment, regressor_square, regressor_weight = adam_update(regressor, regressor_grad, regressor_first, regressor_second, RATE_WEIGHT, DECAY)
    return (word_out(word_grad), word_out(word_moment), word_out(word_square), word_out(word_weight), tables_grad, tables_moment, tables_square, tables_weight, block_out(matrices_grad), block_out(matrices_moment), block_out(matrices_square), block_out(matrices_weight), vectors_grad, vectors_moment, vectors_square, vectors_weight, regressor_grad, regressor_moment, regressor_square, regressor_weight, grad_norm, loss_total, task_counts)
```

```python
import functools

import jax
import jax.numpy as jnp
from jax import lax
from jax.experimental import pallas as pl
from jax.experimental.pallas import tpu as pltpu
from jax.sharding import PartitionSpec as P

HEAD = 64
STEP = 5


HIGHEST = lax.Precision.HIGHEST
FLOAT = jnp.float32
BFLOAT = jnp.bfloat16
NORM_EPS = 1e-12
CLIP = 0.05
BETA_ONE = 0.9
BETA_TWO = 0.999
ADAM_EPS = 1e-08
RATE_WEIGHT = 0.03
RATE_VECTOR = 0.3
DECAY = 0.01


def layer_norm(inputs, norm_gain, norm_bias):
    center = jnp.mean(inputs, axis=-1, keepdims=True)
    offset = inputs - center
    spread = jnp.mean(offset * offset, axis=-1, keepdims=True)
    return offset * lax.rsqrt(spread + NORM_EPS) * norm_gain + norm_bias


def gelu_exact(inputs):
    return jax.nn.gelu(inputs, approximate=False)


MIB = 1 << 20
CHEAP = pl.CostEstimate(flops=1, bytes_accessed=1, transcendentals=0)
ROOT_HALF = 0.5**0.5
BELL = (2.0 * 3.141592653589793) ** -0.5
CONTRACT_LAST = (((1,), (1,)), ((), ()))
CONTRACT_FIRST = (((0,), (0,)), ((), ()))
CONTRACT_CROSS = (((0,), (1,)), ((), ()))


def matmul(left, right, dims=(((1,), (0,)), ((), ()))):
    return lax.dot_general(left, right, dims, preferred_element_type=FLOAT)


def softmax_down(query, keys):
    scores = matmul(keys, query, CONTRACT_LAST) * HEAD ** (-0.5)
    powers = jnp.exp(scores - jnp.max(scores, axis=0, keepdims=True))
    return powers * (1.0 / jnp.sum(powers, axis=0, keepdims=True))


def add_over_steps(step, out_ref, part):
    @pl.when(step == 0)
    def _():
        out_ref[0] = part

    @pl.when(step > 0)
    def _():
        out_ref[0] = out_ref[0] + part


def attention_forward_kernel(order_ref, low_ref, weight_ref, bias_ref, saved_ref, attended_ref):
    width = weight_ref.shape[2] // 4
    heads = width // HEAD
    cut, pad = 3 * width - HEAD, HEAD
    projected = matmul(low_ref[0], weight_ref[0]) + bias_ref[0]
    low = projected.astype(BFLOAT)
    parts = [jnp.zeros((pad, low.shape[0]), FLOAT)]
    for head in range(heads):
        query, keys, values = [
            low[:, c * width + head * HEAD : c * width + (head + 1) * HEAD] for c in range(3)
        ]
        weights = softmax_down(query, keys).astype(BFLOAT)
        parts.append(matmul(values, weights, CONTRACT_FIRST))
    context = jnp.concatenate(parts, axis=0).T.astype(BFLOAT)
    lane = lax.broadcasted_iota(jnp.int32, context.shape, 1)
    saved_ref[0, 0, :, :cut] = low[:, :cut]
    saved_ref[0, 0, :, cut:] = jnp.where(lane < pad, low[:, cut:], context)
    add_over_steps(
        pl.program_id(1), attended_ref, matmul(context, weight_ref[0, :, cut:], CONTRACT_LAST)
    )


def norm_parts(values):
    center = jnp.mean(values, axis=-1, keepdims=True)
    offset = values - center
    inverse = lax.rsqrt(jnp.mean(offset * offset, axis=-1, keepdims=True) + NORM_EPS)
    return offset * inverse, inverse


def norm_back(normed, inverse, gain, grad):
    scaled = grad * gain
    mean = jnp.mean(scaled, axis=-1, keepdims=True)
    along = jnp.mean(scaled * normed, axis=-1, keepdims=True)
    sums = [jnp.sum(grad * normed, axis=0, keepdims=True), jnp.sum(grad, axis=0, keepdims=True)]
    return inverse * (scaled - mean - normed * along), sums


def store_rows(out_ref, rows):
    out_ref[0] = jnp.zeros(out_ref.shape[1:], FLOAT)
    for index, row in enumerate(rows):
        out_ref[0, index : index + 1] = row


def store_half(step, other_ref, own_ref, value, total_ref):
    for index in range(2):

        @pl.when(step == index)
        def _():
            other_ref[index][0] = value

    @pl.when(step >= 2)
    def _():
        own_ref[0, 0] = value

    if total_ref is not None:
        total = jnp.sum(value.astype(FLOAT), axis=0, keepdims=True)
        total_ref[0, 0] = jnp.broadcast_to(total, total_ref.shape[2:])


def add_step(step, sum_ref, part):
    @pl.when(step == 0)
    def _():
        sum_ref[...] = part

    @pl.when(step > 0)
    def _():
        sum_ref[...] = sum_ref[...] + part


def attention_backward_kernel(
    order_ref, saved_ref, weight_ref, grad_ref, residual_ref, embedded_ref, segment_ref, vector_ref,
    other0_ref, other1_ref, own_ref, total_ref, words_ref, tables_ref, sums_ref, through,
):
    width = weight_ref.shape[2] // 4
    heads = width // HEAD
    cut, pad = 3 * width - HEAD, HEAD
    low = saved_ref[0, 0]
    grad_context = matmul(grad_ref[0], weight_ref[0, :, cut:]).astype(BFLOAT)
    grads = [[], [], []]
    for head in range(heads):
        query, keys, values = [
            low[:, c * width + head * HEAD : c * width + (head + 1) * HEAD] for c in range(3)
        ]
        grad_head = grad_context[:, pad + head * HEAD : pad + (head + 1) * HEAD]
        probs = softmax_down(query, keys)
        grad_weights = matmul(values, grad_head, CONTRACT_LAST)
        weighted = probs * grad_weights
        total = jnp.sum(weighted, axis=0, keepdims=True)
        grad_scores = (weighted - probs * total).astype(BFLOAT)
        grads[0].append(matmul(keys, grad_scores, CONTRACT_FIRST) * HEAD ** (-0.5))
        grads[1].append(matmul(query, grad_scores, CONTRACT_CROSS) * HEAD ** (-0.5))
        grads[2].append(matmul(grad_head, probs.astype(BFLOAT), CONTRACT_CROSS))
    blank = [jnp.zeros((pad, low.shape[0]), FLOAT)]
    turned = jnp.concatenate(grads[0] + grads[1] + grads[2] + blank, axis=0).T.astype(BFLOAT)
    span = 3 * width + pad
    lane = lax.broadcasted_iota(jnp.int32, (low.shape[0], 4 * width - cut), 1)
    tail = jnp.concatenate([turned[:, cut:], low[:, span:]], axis=1)
    tail = jnp.where(lane < pad, tail, low[:, cut:])
    step = pl.program_id(1)
    store_half(step, (other0_ref, other1_ref), own_ref, jnp.concatenate([turned[:, :cut], tail], axis=1), total_ref)
    add_step(step, through, matmul(turned, weight_ref[0, :, :span], CONTRACT_LAST))

    @pl.when(step == pl.num_programs(1) - 1)
    def _():
        normed, inverse = norm_parts(embedded_ref[0])
        grad = residual_ref[0] + through[...]
        grad_embedded, rows = norm_back(normed, inverse, vector_ref[0:1], grad)
        grad_low = grad_embedded.astype(BFLOAT)
        for group in range(words_ref.shape[0]):
            words_ref[group, 0] = grad_low[:, group * width : (group + 1) * width]
        second = segment_ref[0].astype(FLOAT)
        rows.append(jnp.sum(grad_embedded * (1.0 - second), axis=0, keepdims=True))
        rows.append(jnp.sum(grad_embedded * second, axis=0, keepdims=True))
        store_rows(sums_ref, rows)
        add_step(pl.program_id(0), tables_ref, grad_embedded)


def feed_forward_kernel(
    order_ref, zero_ref, attended_ref, up_ref, down_ref, bias_ref, vector_ref, head_ref, target_ref,
    other0_ref, other1_ref, own_ref, slope_ref, residual_ref, low_ref, grad_ref, grad_low_ref, sums_ref,
    hidden, fed,
):
    step = pl.program_id(1)

    @pl.when(step == 0)
    def _():
        residual = zero_ref[0] + (attended_ref[0] + vector_ref[4:5])
        residual_ref[0] = residual
        hidden[...] = norm_parts(residual)[0] * vector_ref[5:6] + vector_ref[6:7]
        low_ref[0] = hidden[...].astype(BFLOAT)

    inner = matmul(low_ref[0], up_ref[0]) + bias_ref[0]
    share = 0.5 + 0.5 * lax.erf(inner * ROOT_HALF)
    slope_ref[0, 0] = share + inner * (BELL * jnp.exp(-0.5 * inner * inner))
    active = (inner * share).astype(BFLOAT)
    store_half(step, (other0_ref, other1_ref), own_ref, active, None)
    add_step(step, fed, matmul(active, down_ref[0], CONTRACT_LAST))

    @pl.when(step == pl.num_programs(1) - 1)
    def _():
        normed, inverse = norm_parts(hidden[...] + (fed[...] + vector_ref[11:12]))
        hidden_two = normed * vector_ref[12:13] + vector_ref[13:14]
        row = head_ref[0, 0:1]
        predicted = jnp.sum(hidden_two * row, axis=1, keepdims=True)
        errors = (predicted - target_ref[0, :, 0:1]) * target_ref[0, :, 1:2]
        grad_predicted = errors * head_ref[0, 1:2, 0:1]
        grad_residual, rows = norm_back(normed, inverse, vector_ref[12:13], grad_predicted * row)
        grad_ref[0] = grad_residual
        grad_low = grad_residual.astype(BFLOAT)
        grad_low_ref[0] = grad_low
        rows.append(jnp.sum(grad_low.astype(FLOAT), axis=0, keepdims=True))
        rows.append(jnp.sum(grad_predicted * hidden_two, axis=0, keepdims=True))
        squares = jnp.sum(errors * errors, axis=0, keepdims=True)
        rows.append(jnp.broadcast_to(squares, rows[0].shape))
        store_rows(sums_ref, rows)


def feed_backward_kernel(
    order_ref, grad_low_ref, slope_ref, up_ref, down_ref, grad_ref, residual_ref, vector_ref,
    other0_ref, other1_ref, own_ref, total_ref, grad_one_ref, grad_one_low_ref, sums_ref, through,
):
    grad_active = matmul(grad_low_ref[0], down_ref[0])
    grad_inner = (grad_active * slope_ref[0, 0]).astype(BFLOAT)
    step = pl.program_id(1)
    store_half(step, (other0_ref, other1_ref), own_ref, grad_inner, total_ref)
    add_step(step, through, matmul(grad_inner, up_ref[0], CONTRACT_LAST))

    @pl.when(step == pl.num_programs(1) - 1)
    def _():
        normed, inverse = norm_parts(residual_ref[0])
        grad = grad_ref[0] + through[...]
        grad_residual, rows = norm_back(normed, inverse, vector_ref[5:6], grad)
        grad_one_ref[0] = grad_residual
        grad_low = grad_residual.astype(BFLOAT)
        grad_one_low_ref[0] = grad_low
        rows.append(jnp.sum(grad_low.astype(FLOAT), axis=0, keepdims=True))
        store_rows(sums_ref, rows)


def over_groups(body, order, inputs, outputs, scratch=()):
    examples, length, _ = next(value for kind, value in inputs if kind == "rows").shape

    def spec(kind, shape):
        if kind == "whole":
            return pl.BlockSpec(shape, lambda e, j, o: (0,) * len(shape))
        if kind == "words":
            return pl.BlockSpec((shape[0], 1) + shape[2:], lambda e, j, o: (0, e, 0, 0))
        if kind == "rows":
            return pl.BlockSpec((1,) + shape[1:], lambda e, j, o: (e, 0, 0))
        if kind == "group":
            return pl.BlockSpec((1,) + shape[1:], lambda e, j, o: (o[j], 0, 0))
        if kind in ("group left", "group right"):
            side = int(kind == "group right")
            return pl.BlockSpec(
                (1, shape[1], shape[2] // 2), lambda e, j, o, side=side: (o[j], 0, side)
            )
        if kind == "steps":
            return pl.BlockSpec((1, 1) + shape[2:], lambda e, j, o: (j, e, 0, 0))
        return pl.BlockSpec((1, 1) + shape[2:], lambda e, j, o: (jnp.maximum(j - 2, 0), e, 0, 0))

    return pl.pallas_call(
        body,
        grid_spec=pltpu.PrefetchScalarGridSpec(
            num_scalar_prefetch=1,
            grid=(examples, order.shape[0]),
            in_specs=[spec(kind, value.shape) for kind, value in inputs],
            out_specs=[spec(kind, value.shape) for kind, value in outputs],
            scratch_shapes=scratch,
        ),
        out_shape=[value for _, value in outputs],
        compiler_params=pltpu.CompilerParams(vmem_limit_bytes=56 * MIB),
        cost_estimate=pl.CostEstimate(flops=1, bytes_accessed=1, transcendentals=0),
    )(order, *[value for _, value in inputs])


X_BIT = 0


def place_of_piece(order, relative):
    index, weight = 0, 0
    for bit in order[1:]:
        index *= 2
        weight *= 2
        if bit == X_BIT:
            weight = 1
        else:
            index += int(bool(relative & bit))
    return bool(relative & order[0]), index, weight


def task_outer_kernel(pairs, mixed, orders, place_ref, *refs):
    count = (3 if mixed else 2) * pairs + 1
    inputs, outputs, sums = refs[:count], refs[count:-1], refs[-1]
    tasks, rows, width = sums.shape
    examples = inputs[0].shape[0]
    blocks = outputs[0].shape[0]
    block = outputs[0].shape[2]
    half = width // 2
    split = 3 * width // 4
    aligned = split // 256 * 256
    sums[...] = jnp.zeros_like(sums)
    for pair in range(pairs):
        left_ref = inputs[pair]
        for example in range(examples):
            task = place_ref[pair * examples + example]
            if pair == 0:
                right = inputs[pairs][0, example]
            else:
                right = jnp.where(
                    pl.program_id(0) == 0, inputs[pairs + 1][example], inputs[pairs + 2][example]
                )
            product = matmul(left_ref[example], right, CONTRACT_FIRST)
            if mixed:
                tail = matmul(inputs[2 * pairs + 1 + pair][example], right[:, aligned:], CONTRACT_FIRST)
                lane = lax.broadcasted_iota(jnp.int32, tail.shape, 1) + aligned
                tail = jnp.where(lane >= split, tail, product[:, aligned:])
                sums[task, :, :aligned] = sums[task, :, :aligned] + product[:, :aligned]
                sums[task, :, aligned:] = sums[task, :, aligned:] + tail
            else:
                sums[task] = sums[task] + product
    step = pl.program_id(0)
    own = place_ref[pairs * examples]

    def store(ref, index, task, part):
        ref[index, task] = part

    for relative in range(blocks):
        start = pl.multiple_of(lax.bitwise_xor(own, relative) * block, 8)
        for task in range(tasks):
            part = sums[task, pl.ds(start, block), :].astype(BFLOAT)
            for side, order in enumerate(orders):
                send_ref, keep_ref = outputs[2 * side : 2 * side + 2]
                piece = part[:, side * half : (side + 1) * half]
                sent, index, weight = place_of_piece(order, relative)
                if order[0] == X_BIT:
                    pl.when(step == 0)(functools.partial(store, send_ref, index, task, piece))
                    pl.when(step == 1)(functools.partial(store, keep_ref, index, task, piece))
                else:
                    store(send_ref if sent else keep_ref, index + (1 - step) * weight, task, piece)


def task_outer(place, lefts, rights, tasks, blocks, orders, others=()):
    examples, length, rows = lefts[0].shape
    width = rights[0].shape[3]
    pairs = len(lefts)
    once = pl.BlockSpec((examples, length, rows), lambda s, p: (0, 0, 0), pipeline_mode=pl.Buffered(1))
    right_spec = pl.BlockSpec((1, examples, length, width), lambda s, p: (s, 0, 0, 0))
    right_once = pl.BlockSpec((examples, length, width), lambda s, p: (0, 0, 0), pipeline_mode=pl.Buffered(1))
    shape = (blocks, tasks, rows // blocks, width // 2)
    out = jax.ShapeDtypeStruct(shape, BFLOAT)
    whole = pl.BlockSpec(shape, lambda s, p: (0, 0, 0, 0), pipeline_mode=pl.Buffered(1))
    sent0, kept0, sent1, kept1 = pl.pallas_call(
        functools.partial(task_outer_kernel, pairs, bool(others), orders),
        grid_spec=pltpu.PrefetchScalarGridSpec(
            num_scalar_prefetch=1,
            grid=(2,),
            in_specs=[once] * pairs + [right_spec, right_once, right_once] + [once] * len(others),
            out_specs=[whole] * 4,
            scratch_shapes=[pltpu.VMEM((tasks, rows, width), FLOAT)],
        ),
        out_shape=[out] * 4,
        compiler_params=pltpu.CompilerParams(vmem_limit_bytes=58 * MIB),
        cost_estimate=CHEAP,
    )(place, *lefts, *rights, *others)
    return [(sent0, kept0), (sent1, kept1)]


BLOCK = 128


def distinct_kernel(rows_owner, owners, round_ref, ids_ref, rank_ref, slot_ref, wanted_ref, held, total):
    count = ids_ref.shape[1]
    slots = wanted_ref.shape[1] // owners
    blocks = count // BLOCK

    def down(row):
        return jnp.broadcast_to(row, (BLOCK, BLOCK)).T

    def fold(tile):
        return jnp.sum(tile.reshape(BLOCK // 8, 8, BLOCK), axis=0)

    def sweep(term, targets, *rows):
        total[...] = jnp.zeros_like(total)

        def step(k, carry):
            start = pl.multiple_of(k * BLOCK, BLOCK)
            columns = [down(row[:, pl.ds(start, BLOCK)]) for row in rows]
            for block in range(targets):
                lanes = slice(block * BLOCK, (block + 1) * BLOCK)
                total[:, lanes] = total[:, lanes] + fold(term(columns, start, lanes))
            return carry

        lax.fori_loop(0, blocks, step, 0)
        return jnp.sum(total[...], axis=0, keepdims=True)

    place = lax.broadcasted_iota(jnp.int32, (BLOCK, BLOCK), 0) - lax.broadcasted_iota(
        jnp.int32, (BLOCK, BLOCK), 1
    )
    ids = ids_ref[...]

    total[...] = jnp.zeros_like(total)

    def earlier(k, carry):
        lanes = pl.ds(pl.multiple_of(k * BLOCK, BLOCK), BLOCK)
        column = down(ids_ref[:, lanes])
        same = (column == ids_ref[:, lanes]) & (place < 0)
        total[:, lanes] = total[:, lanes] + fold(jnp.where(same, 1.0, 0.0))

        def later(j, carry):
            lanes = pl.ds(pl.multiple_of(j * BLOCK, BLOCK), BLOCK)
            total[:, lanes] = total[:, lanes] + fold(jnp.where(column == ids_ref[:, lanes], 1.0, 0.0))
            return carry

        return lax.fori_loop(k + 1, blocks, later, carry)

    lax.fori_loop(0, blocks, earlier, 0)
    first = jnp.sum(total[...], axis=0, keepdims=True) == 0.0
    far = float(owners * rows_owner)
    held[0:1] = jnp.where(first, ids, far)

    def below(columns, start, lanes):
        return jnp.where(columns[0] < ids_ref[:, lanes], 1.0, 0.0)

    rank = sweep(below, blocks, held.at[0:1])
    owner = jnp.zeros_like(ids)
    start_before = jnp.zeros((1, 1), FLOAT)
    for index in range(1, owners):
        start_here = jnp.sum(
            jnp.where(held[0:1] < float(index * rows_owner), 1.0, 0.0), axis=1, keepdims=True
        )
        reached = ids >= float(index * rows_owner)
        owner = owner + jnp.where(reached, 1.0, 0.0)
        rank = rank - jnp.where(reached, start_here - start_before, 0.0)
        start_before = start_here
    rank_ref[...] = rank.astype(jnp.int32)
    turn = rank - (round_ref[0] * slots).astype(FLOAT)
    taken = (turn >= 0.0) & (turn < float(slots))
    slot = jnp.where(taken, owner * float(slots) + turn, -1.0)
    slot_ref[...] = slot.astype(jnp.int32)
    held[0:1] = jnp.where(first, slot, -1.0)
    held[1:2] = ids - owner * float(rows_owner) + 1.0

    lane = lax.broadcasted_iota(jnp.int32, (1, BLOCK), 1)

    def asked(columns, start, lanes):
        wanted = (lane + lanes.start).astype(FLOAT)
        return jnp.where(columns[0] == wanted, columns[1], 0.0)

    asked_count = wanted_ref.shape[1]
    summed = sweep(asked, asked_count // BLOCK, held.at[0:1], held.at[1:2])
    wanted_ref[...] = (summed[:, :asked_count] - 1.0).astype(jnp.int32)


def distinct(turn, ids, rows_owner, owners, slots):
    count = ids.shape[0]
    whole = pl.BlockSpec((1, count), lambda i, turn: (0, 0))
    asked = pl.BlockSpec((1, owners * slots), lambda i, turn: (0, 0))
    out = jax.ShapeDtypeStruct((1, count), jnp.int32)
    values = pl.pallas_call(
        functools.partial(distinct_kernel, rows_owner, owners),
        grid_spec=pltpu.PrefetchScalarGridSpec(
            num_scalar_prefetch=1,
            grid=(1,),
            in_specs=[whole],
            out_specs=[whole, whole, asked],
            scratch_shapes=[pltpu.VMEM((8, count), FLOAT), pltpu.VMEM((8, count), FLOAT)],
        ),
        out_shape=[out, out, jax.ShapeDtypeStruct((1, owners * slots), jnp.int32)],
        compiler_params=pltpu.CompilerParams(vmem_limit_bytes=32 * MIB),
        cost_estimate=pl.CostEstimate(flops=1, bytes_accessed=1, transcendentals=0),
    )(jnp.reshape(turn, (1,)).astype(jnp.int32), ids.astype(FLOAT).reshape(1, count))
    return [value.reshape(-1) for value in values]


def match_kernel(left_ref, right_ref, rows_ref, out_ref):
    hot = jnp.where(left_ref[...] == right_ref[...], 1.0, 0.0).astype(BFLOAT)
    out_ref[...] = matmul(hot, rows_ref[...]).astype(out_ref.dtype)


def match_pairs_kernel(right_ref, rows_ref, out_ref):
    count = out_ref.shape[0]
    left = 2 * (pl.program_id(0) * count + lax.broadcasted_iota(jnp.int32, (count, 1), 0))
    sums = []
    for odd in range(2):
        hot = jnp.where(left + odd == right_ref[...], 1.0, 0.0).astype(BFLOAT)
        sums.append(matmul(hot, rows_ref[...]))
    out_ref[...] = jnp.concatenate(sums, axis=1)


def match_pairs(stored, right, rows):
    count, width = rows.shape
    wide = next(b for b in (240, 120, 80, 40, 24, 16, 8) if stored[0] % b == 0)
    return pl.pallas_call(
        match_pairs_kernel,
        grid=(stored[0] // wide,),
        in_specs=[pl.BlockSpec((1, count), lambda i: (0, 0)), pl.BlockSpec((count, width), lambda i: (0, 0))],
        out_specs=pl.BlockSpec((wide, 2 * width), lambda i: (i, 0)),
        out_shape=jax.ShapeDtypeStruct(stored, FLOAT),
        compiler_params=pltpu.CompilerParams(vmem_limit_bytes=48 * MIB),
        cost_estimate=CHEAP,
    )(right.reshape(1, -1), rows)


def match_rows(left, right, rows, dtype):
    count, width = rows.shape
    wide = next(b for b in (512, 480, 256, 240, 128, 64, 32, 16) if left.shape[0] % b == 0)
    return pl.pallas_call(
        match_kernel,
        grid=(left.shape[0] // wide,),
        in_specs=[
            pl.BlockSpec((wide, 1), lambda i: (i, 0)),
            pl.BlockSpec((1, count), lambda i: (0, 0)),
            pl.BlockSpec((count, width), lambda i: (0, 0)),
        ],
        out_specs=pl.BlockSpec((wide, width), lambda i: (i, 0)),
        out_shape=jax.ShapeDtypeStruct((left.shape[0], width), dtype),
        compiler_params=pltpu.CompilerParams(vmem_limit_bytes=48 * MIB),
        cost_estimate=pl.CostEstimate(flops=1, bytes_accessed=1, transcendentals=0),
    )(left.reshape(-1, 1), right.reshape(1, -1), rows)


def swap(value, axis, bit):
    size = lax.axis_size(axis)
    return lax.ppermute(value, axis, [(i, i ^ bit) for i in range(size)])


def hop(value, bit):
    return swap(value, "mp", 2) if bit == X_BIT else swap(value, "dp", bit)


def first_hop(pieces, orders):
    return [(keep, hop(send, order[0])) for (send, keep), order in zip(pieces, orders)]


def next_sums_kernel(own_ref, came_ref, own_far_ref, came_far_ref, keep_ref, send_ref):
    keep_ref[...] = own_ref[...].astype(FLOAT) + came_ref[...].astype(FLOAT)
    send_ref[...] = (own_far_ref[...].astype(FLOAT) + came_far_ref[...].astype(FLOAT)).astype(BFLOAT)


def next_sums(state):
    own, came = state
    shape = own.shape
    half = shape[0] // 2
    near = pl.BlockSpec((1,) + shape[1:], lambda i: (i, 0, 0, 0))
    far = pl.BlockSpec((1,) + shape[1:], lambda i: (i + half, 0, 0, 0))
    return pl.pallas_call(
        next_sums_kernel,
        grid=(half,),
        in_specs=[near, near, far, far],
        out_specs=[near, near],
        out_shape=[jax.ShapeDtypeStruct((half,) + shape[1:], kind) for kind in (FLOAT, BFLOAT)],
        cost_estimate=CHEAP,
    )(own, came, own, came)


class Reduction:
    def __init__(self):
        self.states, self.orders, self.done, self.last = {}, {}, {}, None

    def begin(self, group, pieces, orders):
        for half, ((send, keep), order) in enumerate(zip(pieces, orders)):
            self.states[group, half] = (keep, hop(send, order[0]))
            self.orders[group, half] = order
            self.done[group, half] = 1

    def tie(self, key, value):
        own, came = self.states[key]
        own, value = lax.optimization_barrier((own, value))
        self.states[key] = (own, came)
        return value

    def advance(self, *keys):
        for key in keys:
            own, came = self.states[key]
            if self.last is not None and self.last != key:
                own = self.tie(self.last, own)
            keep, send = next_sums((own, came))
            self.states[key] = (keep, hop(send, self.orders[key][self.done[key]]))
            self.done[key] += 1
            self.last = key

    def complete(self, group):
        keys = [(group, 0), (group, 1)]
        for key in keys:
            while self.done[key] < len(self.orders[key]):
                self.advance(key)
        return finish_group([self.states[key] for key in keys])


def part_of(rows):
    return -(-rows // 32) * 8


def store_halves(side, keep_ref, send_ref, value):
    half = keep_ref.shape[0]
    for index in range(2):
        piece = value[index * half : (index + 1) * half]

        @pl.when(side == index)
        def _():
            keep_ref[...] = piece

        @pl.when(side != index)
        def _():
            send_ref[...] = piece


def collect_kernel(place_ref, tables_ref, zero_ref, one_ref, two_ref, inner_ref, mixed_ref, keep_ref, send_ref, rows_ref):
    groups, examples, _, width = inner_ref.shape
    length = tables_ref.shape[0]
    column = width // 4

    def summed(ref, row):
        return sum(ref[e, row : row + 1] for e in range(examples))

    def natural(ref, block):
        parts = []
        for group in range(groups):
            step = place_ref[group]
            row = sum(ref[step, e, 0:1] for e in range(examples))
            parts.append(row[:, block * column : (block + 1) * column])
        return jnp.concatenate(parts, axis=1)

    rows_ref[length:] = jnp.zeros((rows_ref.shape[0] - length, rows_ref.shape[1]), FLOAT)
    rows_ref[:length] = tables_ref[...]
    rows = [summed(zero_ref, 2), summed(zero_ref, 3), summed(zero_ref, 0), summed(zero_ref, 1)]
    rows += [natural(mixed_ref, 0), natural(mixed_ref, 2), summed(one_ref, 2), summed(one_ref, 0), summed(one_ref, 1)]
    rows += [natural(inner_ref, block) for block in range(4)]
    rows += [summed(two_ref, 2), summed(two_ref, 0), summed(two_ref, 1)]
    for index, row in enumerate(rows):
        rows_ref[length + index : length + index + 1] = row
    first = length + len(rows)
    for example in range(examples):
        task = place_ref[groups + example]
        at = pl.ds(first + task, 1)
        rows_ref[at] = rows_ref[at] + two_ref[example, 3:4]
    store_halves(place_ref[groups + examples], keep_ref, send_ref, rows_ref)


def collect(place, tables, zero, one, two, inner, mixed, rows):
    half = jax.ShapeDtypeStruct((2 * part_of(rows), tables.shape[1]), FLOAT)
    return pl.pallas_call(
        collect_kernel,
        grid_spec=pltpu.PrefetchScalarGridSpec(
            num_scalar_prefetch=1,
            grid=(1,),
            in_specs=[
                pl.BlockSpec(v.shape, lambda i, p, d=len(v.shape): (0,) * d)
                for v in (tables, zero, one, two, inner, mixed)
            ],
            out_specs=[pl.BlockSpec(half.shape, lambda i, p: (0, 0))] * 2,
            scratch_shapes=[pltpu.VMEM((2 * half.shape[0], half.shape[1]), FLOAT)],
        ),
        out_shape=[half, half],
        compiler_params=pltpu.CompilerParams(vmem_limit_bytes=32 * MIB),
        cost_estimate=CHEAP,
    )(place, tables, zero, one, two, inner, mixed)


def small_call(body, side, values, outputs):
    def whole(value):
        return pl.BlockSpec(value.shape, lambda i, p, d=len(value.shape): (0,) * d)

    return pl.pallas_call(
        body,
        grid_spec=pltpu.PrefetchScalarGridSpec(
            num_scalar_prefetch=1,
            grid=(1,),
            in_specs=[whole(v) for v in values],
            out_specs=[whole(v) for v in outputs],
        ),
        out_shape=outputs,
        compiler_params=pltpu.CompilerParams(vmem_limit_bytes=32 * MIB),
        cost_estimate=CHEAP,
    )(jnp.reshape(side, (1,)).astype(jnp.int32), *values)


def add_rows_kernel(side_ref, own_ref, came_ref, keep_ref, send_ref):
    store_halves(side_ref[0], keep_ref, send_ref, own_ref[...] + came_ref[...])


def add_columns_kernel(side_ref, own_ref, came_ref, keep_ref, send_ref):
    total = own_ref[...] + came_ref[...]
    width = keep_ref.shape[2]
    for index in range(2 * keep_ref.shape[0]):
        piece = total[:, index * width : (index + 1) * width]

        @pl.when(side_ref[0] == index % 2)
        def _():
            keep_ref[index // 2] = piece

        @pl.when(side_ref[0] != index % 2)
        def _():
            send_ref[index // 2] = piece


def add_blocks_kernel(side_ref, own_ref, came_ref, keep_ref, send_ref):
    for index in range(2 * keep_ref.shape[0]):
        piece = own_ref[index] + came_ref[index]

        @pl.when(side_ref[0] == index % 2)
        def _():
            keep_ref[index // 2] = piece

        @pl.when(side_ref[0] != index % 2)
        def _():
            send_ref[index // 2] = piece


def add_last_kernel(side_ref, own_ref, came_ref, out_ref):
    out_ref[...] = own_ref[0] + came_ref[0]


def join_kernel(side_ref, own_ref, came_ref, out_ref):
    half = own_ref.shape[0]
    for index in range(2):
        rows = slice(index * half, (index + 1) * half)

        @pl.when(side_ref[0] == index)
        def _():
            out_ref[rows] = own_ref[...]

        @pl.when(side_ref[0] != index)
        def _():
            out_ref[rows] = came_ref[...]


def embed_kernel(words_ref, tables_ref, segment_ref, scale_ref, embedded_ref, normed_ref, low_ref):
    length = embedded_ref.shape[1]
    words = jnp.concatenate([words_ref[m, 0] for m in range(words_ref.shape[0])], axis=1).astype(FLOAT)
    part = jnp.where(segment_ref[0] == 1, tables_ref[length + 1 : length + 2], tables_ref[length : length + 1])
    embedded = words + tables_ref[:length] + part
    embedded_ref[0] = embedded
    normed = layer_norm(embedded, scale_ref[0:1], scale_ref[1:2])
    normed_ref[0] = normed
    low_ref[0] = normed.astype(BFLOAT)


def embed(words, table_rows, segments, scales):
    groups, examples, length, width = words.shape
    full = groups * width
    rows = pl.BlockSpec((1, length, full), lambda e: (e, 0, 0))
    return pl.pallas_call(
        embed_kernel,
        cost_estimate=CHEAP,
        grid=(examples,),
        in_specs=[
            pl.BlockSpec((groups, 1, length, width), lambda e: (0, e, 0, 0)),
            pl.BlockSpec(table_rows.shape, lambda e: (0, 0)),
            pl.BlockSpec((1, length, 1), lambda e: (e, 0, 0)),
            pl.BlockSpec(scales.shape, lambda e: (0, 0)),
        ],
        out_specs=[rows, rows, rows],
        out_shape=[
            jax.ShapeDtypeStruct((examples, length, full), kind) for kind in (FLOAT, FLOAT, BFLOAT)
        ],
        compiler_params=pltpu.CompilerParams(vmem_limit_bytes=48 * MIB),
    )(words, table_rows, segments[:, :, None], scales)


LANES = 128


def finish_group_kernel(own0_ref, came0_ref, own1_ref, came1_ref, total_ref, gram_ref):
    tasks = own0_ref.shape[1]
    half = own0_ref.shape[3]
    for task in range(tasks):
        total_ref[task, :, :half] = own0_ref[0, task] + came0_ref[0, task].astype(FLOAT)
        total_ref[task, :, half:] = own1_ref[0, task] + came1_ref[0, task].astype(FLOAT)
    lane = lax.broadcasted_iota(jnp.int32, gram_ref.shape, 1)
    gram = jnp.zeros(gram_ref.shape, FLOAT)
    for i in range(tasks):
        for j in range(i, tasks):
            product = jnp.sum(total_ref[i] * total_ref[j], axis=0, keepdims=True)
            product = jnp.sum(product, axis=1, keepdims=True)
            gram = gram + jnp.where((lane == i * tasks + j) | (lane == j * tasks + i), product, 0.0)
    gram_ref[...] = gram


def finish_group(states):
    _, tasks, rows, half = states[0][0].shape
    return pl.pallas_call(
        finish_group_kernel,
        out_shape=[
            jax.ShapeDtypeStruct((tasks, rows, 2 * half), FLOAT),
            jax.ShapeDtypeStruct((1, LANES), FLOAT),
        ],
        compiler_params=pltpu.CompilerParams(vmem_limit_bytes=32 * MIB),
        cost_estimate=CHEAP,
    )(*states[0], *states[1])


def adam_update(weight, gradient, first_moment, second_moment, step_rate, weight_decay):
    moment_new = BETA_ONE * first_moment + (1.0 - BETA_ONE) * gradient
    square_new = BETA_TWO * second_moment + (1.0 - BETA_TWO) * gradient * gradient
    corrected = moment_new / (1.0 - BETA_ONE**STEP)
    scaled = square_new / (1.0 - BETA_TWO**STEP)
    weight_new = weight - step_rate * (
        corrected / (jnp.sqrt(scaled) + ADAM_EPS) + weight_decay * weight
    )
    return (moment_new, square_new, weight_new)


def update_kernel(sizes, order_ref, scalar_ref, count_ref, *refs):
    tasks, tables_end, vectors_end = sizes
    small_ref, word_grad_ref, *refs = refs
    groups, refs = refs[:3], refs[3:]
    inputs, outputs, report_ref = refs[:15], refs[15:35], refs[35]
    step = pl.program_id(0)

    def scalar(ref, index):
        return jnp.full((1, 1), ref[0, index], FLOAT)

    gram = [[scalar(scalar_ref, i * tasks + j) for j in range(tasks)] for i in range(tasks)]
    mix = [jnp.zeros((1, 1), FLOAT)] * tasks
    for first in range(tasks):
        current = [jnp.full((1, 1), float(k == first), FLOAT) for k in range(tasks)]
        for position in range(tasks):
            other = order_ref[0, position]
            row = [scalar(scalar_ref, other * tasks + k) for k in range(tasks)]
            dot = sum(current[k] * row[k] for k in range(tasks))
            square = scalar(scalar_ref, other * tasks + other)
            factor = jnp.where(other == first, 0.0, jnp.minimum(dot, 0.0) / square)
            current = [current[k] - jnp.where(other == k, factor, 0.0) for k in range(tasks)]
        mix = [mix[k] + current[k] for k in range(tasks)]
    squares = scalar(scalar_ref, tasks * tasks)
    for i in range(tasks):
        for j in range(tasks):
            squares = squares + mix[i] * mix[j] * gram[i][j]
    norm = jnp.sqrt(squares)
    scale = jnp.minimum(1.0, CLIP / norm)
    loss = sum(scalar(scalar_ref, tasks * tasks + 1 + t) / scalar(count_ref, t) for t in range(tasks))
    lane = lax.broadcasted_iota(jnp.int32, report_ref.shape, 1)
    report_ref[...] = jnp.where(lane == 0, norm, loss)

    def update(index, gradient, rate, decay):
        weight_ref, first_ref, second_ref = inputs[3 * index : 3 * index + 3]
        clipped = gradient * scale
        values = adam_update(weight_ref[...], clipped, first_ref[...], second_ref[...], rate, decay)
        for out_ref, value in zip(outputs[4 * index : 4 * index + 4], (clipped, *values)):
            out_ref[...] = value

    update(0, word_grad_ref[...], RATE_WEIGHT, DECAY)
    for group, group_ref in enumerate(groups):

        @pl.when(step == group)
        def _():
            update(2, sum(mix[t] * group_ref[t] for t in range(tasks)), RATE_WEIGHT, DECAY)

    @pl.when(step == 0)
    def _():
        update(1, small_ref[:tables_end], RATE_WEIGHT, DECAY)
        update(3, small_ref[tables_end:vectors_end], RATE_VECTOR, 0.0)
        update(4, small_ref[vectors_end : vectors_end + tasks], RATE_WEIGHT, DECAY)


def update_all(order, scalars, counts, small, word_grad, groups, arrays):
    steps = len(groups)
    tasks = groups[0].shape[0]
    tables_end = arrays[3].shape[0]

    def whole(value):
        return pl.BlockSpec(value.shape, lambda i, d=len(value.shape): (0,) * d)

    def spec(index, value):
        rows, width = value.shape
        if index == 0:
            return pl.BlockSpec((rows // steps, width), lambda i: (i, 0))
        if index == 2:
            return pl.BlockSpec((rows, width // steps), lambda i: (0, i))
        return whole(value)

    scalar_spec = pl.BlockSpec(memory_space=pltpu.SMEM)
    report = jax.ShapeDtypeStruct((8, LANES), FLOAT)
    outputs = [(index, arrays[3 * index]) for index in range(5) for _ in range(4)]
    return pl.pallas_call(
        functools.partial(update_kernel, (tasks, tables_end, tables_end + arrays[9].shape[0])),
        grid=(steps,),
        in_specs=[scalar_spec] * 3
        + [whole(small), spec(0, word_grad)]
        + [whole(group) for group in groups]
        + [spec(i // 3, value) for i, value in enumerate(arrays)],
        out_specs=[spec(index, value) for index, value in outputs] + [whole(report)],
        out_shape=[jax.ShapeDtypeStruct(value.shape, FLOAT) for _, value in outputs] + [report],
        compiler_params=pltpu.CompilerParams(vmem_limit_bytes=56 * MIB),
    )(order.reshape(1, -1), scalars, counts.reshape(1, -1), small, word_grad, *groups, *arrays)


def on_device(
    token_ids,
    segment_ids,
    task_ids,
    task_order,
    counted,
    targets,
    word_table,
    word_first,
    word_second,
    tables,
    tables_first,
    tables_second,
    matrices,
    matrices_first,
    matrices_second,
    vectors,
    vectors_first,
    vectors_second,
    regressor,
    regressor_first,
    regressor_second,
):
    word_stored = word_table.shape
    nd = lax.axis_size("dp")
    nm = lax.axis_size("mp")
    m_index = lax.axis_index("mp")
    rows_own, width_all = matrices.shape
    width_own = width_all // 12
    full = rows_own * nd
    quarter = 4 * width_own
    tasks = regressor.shape[0]
    slice_width = tables.shape[1]
    batch, length = token_ids.shape
    own = batch // nm
    tokens = own * length

    def mine(rows):
        return lax.dynamic_slice_in_dim(rows, m_index * own, own, 0)

    rows_owner = word_stored[0] * word_stored[1] // width_own
    token_flat = token_ids.reshape(-1)
    slots = token_flat.shape[0] * 5 // 8 // nd
    task_all_hot = (task_ids[:, None] == jnp.arange(tasks, dtype=jnp.int32)[None, :]).astype(FLOAT)
    counted_all = counted.astype(FLOAT)
    counts_here = jnp.sum(task_all_hot * jnp.sum(counted_all, axis=1)[:, None], axis=0)
    high = jnp.floor(counts_here / 256.0)
    coded = jnp.concatenate([high, counts_here - 256.0 * high])
    coded = jnp.pad(coded, (0, slice_width - coded.shape[0]))[None]
    small = jnp.concatenate([tables, vectors, regressor, coded]).astype(BFLOAT)
    small_all = lax.all_to_all(jnp.broadcast_to(small, (nd, *small.shape)), "dp", 0, 0, tiled=True)
    rank, slot, wanted = distinct(jnp.int32(0), token_flat, rows_owner, nd, slots)

    def exchange(rows):
        return lax.all_to_all(rows.reshape(nd, slots, *rows.shape[1:]), "dp", 0, 0, tiled=True).reshape(rows.shape)

    largest = jnp.broadcast_to(jnp.max(rank), (nd, 1))
    asked = jnp.concatenate([wanted.reshape(nd, slots), largest], axis=1)
    asked, small_all = lax.optimization_barrier((asked, small_all))
    asked = lax.all_to_all(asked, "dp", 0, 0, tiled=True)
    rounds = jnp.max(asked[:, slots]) // slots + 1
    asked = asked[:, :slots].reshape(-1)
    coded_all = small_all[:, -1].astype(FLOAT)
    small_all = small_all[:, :-1].transpose(1, 0, 2).reshape(-1, full)
    task_counts = jnp.sum(256.0 * coded_all[:, :tasks] + coded_all[:, tasks : 2 * tasks], axis=0)
    words_low = word_table.astype(BFLOAT).reshape(-1, width_own)
    matrices_low = matrices.astype(BFLOAT)

    def gather_block(start, stop):
        part = matrices_low[:, start * quarter : stop * quarter]
        return lax.all_gather(part, ("mp", "dp"), axis=0, tiled=True).reshape(nm, full, -1)

    block_a, block_uv = gather_block(0, 1), gather_block(1, 3)
    small_full = small_all.astype(FLOAT)
    table_full = small_full[: length + 2]
    vector_full = small_full[length + 2 : length + 2 + vectors.shape[0]]
    regressor_full = small_full[length + 2 + vectors.shape[0] :]
    masks = (3, 1, 2, 0)
    order = jnp.stack([jnp.bitwise_xor(m_index, mask) for mask in masks])
    place_of = jnp.stack([jnp.bitwise_xor(m_index, m) for m in range(nm)])
    place_of = jnp.take(jnp.array([masks.index(k) for k in range(nm)], jnp.int32), place_of)

    def columns(rows):
        return rows.reshape(-1, nm, width_own).transpose(1, 0, 2).reshape(nm, 1, -1)

    blank = jnp.zeros_like(vector_full[2])
    projection_bias = columns(jnp.stack([vector_full[2], blank, vector_full[3], blank]))
    up_bias = columns(vector_full[7:11])

    task_own = mine(task_ids)
    task_hot = mine(task_all_hot)
    segment_own = mine(segment_ids)
    counted_own = mine(counted_all)
    targets_own = mine(targets)

    owner_rows = jnp.arange(rows_owner, dtype=jnp.int32)
    slot_rows = jnp.arange(nd * slots, dtype=jnp.int32)

    def look_up(slot_now, asked_now):
        came = exchange(match_rows(asked_now, owner_rows, words_low, BFLOAT))
        return match_rows(slot_now, slot_rows, came, BFLOAT)

    def look_up_round(state):
        turn, found = state
        _, slot_now, wanted_now = distinct(turn, token_flat, rows_owner, nd, slots)
        return turn + 1, found + look_up(slot_now, exchange(wanted_now))

    looked = look_up(slot, asked)
    looked = lax.while_loop(lambda state: state[0] < rounds, look_up_round, (jnp.int32(1), looked))[1]
    swapped = lax.all_to_all(looked.reshape(nm, tokens, width_own), "mp", 0, 0, tiled=True)
    embedded, hidden_zero, zero_low = embed(
        swapped.reshape(nm, own, length, width_own), table_full, segment_own, vector_full[0:2]
    )

    rows_type = jax.ShapeDtypeStruct((own, length, full), FLOAT)
    group_low = jax.ShapeDtypeStruct((nm, own, length, quarter), BFLOAT)
    group_type = jax.ShapeDtypeStruct((nm, own, length, quarter), FLOAT)
    half_low = jax.ShapeDtypeStruct((nm // 2, own, length, quarter), BFLOAT)
    rows_low = jax.ShapeDtypeStruct(rows_type.shape, BFLOAT)
    sums_type = jax.ShapeDtypeStruct((own, 8, full), FLOAT)
    step_sums = jax.ShapeDtypeStruct((nm, own, 8, quarter), FLOAT)
    row_scratch = pltpu.VMEM((length, full), FLOAT)
    saved, attended = over_groups(
        attention_forward_kernel,
        order,
        [("rows", zero_low), ("group", block_a), ("group", projection_bias)],
        [("steps", group_low), ("rows", rows_type)],
    )
    regressor_rows = jnp.dot(task_hot, regressor_full, precision=HIGHEST)
    error_scale = 2.0 / jnp.dot(task_hot, task_counts, precision=HIGHEST)
    heads = jnp.stack([regressor_rows, jnp.broadcast_to(error_scale[:, None], regressor_rows.shape)], axis=1)
    active_other, active_far, active_own, slope, residual_one, one_low, grad_two, grad_fed, two_sums = over_groups(
        feed_forward_kernel,
        order,
        [
            ("rows", hidden_zero), ("rows", attended), ("group left", block_uv), ("group right", block_uv),
            ("group", up_bias), ("whole", vector_full), ("rows", heads),
            ("rows", jnp.stack([targets_own, counted_own], axis=-1)),
        ],
        [
            ("rows", rows_low), ("rows", rows_low), ("last", half_low), ("steps", group_type), ("rows", rows_type),
            ("rows", rows_low), ("rows", rows_type), ("rows", rows_low), ("rows", sums_type),
        ],
        [row_scratch, row_scratch],
    )
    local_errors = jnp.sum(task_hot * two_sums[:, 4, 0:1], axis=0)

    d_index = lax.axis_index("dp")
    task_near = lax.dynamic_slice_in_dim(task_ids, jnp.bitwise_xor(m_index, 1) * own, own, 0)
    task_chip = jnp.concatenate([task_own, task_near])
    place = jnp.concatenate([task_chip, jnp.stack([d_index])]).astype(jnp.int32)

    def near(value):
        return swap(value, "mp", 1)

    z_bits = tuple(1 << k for k in range(1, nd.bit_length() - 1))
    early = ((X_BIT, 1) + z_bits, (1, X_BIT) + z_bits)
    late = ((X_BIT, 1) + z_bits, z_bits + (1, X_BIT))
    inner_other, inner_far, inner_own, inner_sums, grad_one, grad_attended, one_sums = over_groups(
        feed_backward_kernel,
        order,
        [
            ("rows", grad_fed), ("steps", slope), ("group left", block_uv), ("group right", block_uv),
            ("rows", grad_two), ("rows", residual_one), ("whole", vector_full),
        ],
        [
            ("rows", rows_low), ("rows", rows_low), ("last", half_low), ("steps", step_sums), ("rows", rows_type),
            ("rows", rows_low), ("rows", sums_type),
        ],
        [row_scratch],
    )
    down_pieces = task_outer(
        place, [grad_fed, near(grad_fed)], [active_own, near(active_other), near(active_far)], tasks, nd, early
    )
    reduction = Reduction()
    reduction.begin("down", down_pieces, early)
    inner_own, down_pieces = lax.optimization_barrier((inner_own, down_pieces))
    up_pieces = task_outer(
        place, [one_low, near(one_low)], [inner_own, near(inner_other), near(inner_far)], tasks, nd, late
    )
    reduction.begin("up", up_pieces, late)
    grad_attended, up_pieces = lax.optimization_barrier((grad_attended, up_pieces))
    mixed_other, mixed_far, mixed_own, mixed_sums, word_rows, table_sums, zero_sums = over_groups(
        attention_backward_kernel,
        order,
        [
            ("steps", saved), ("group", block_a), ("rows", grad_attended), ("rows", grad_one),
            ("rows", embedded), ("rows", segment_own[:, :, None]), ("whole", vector_full),
        ],
        [
            ("rows", rows_low), ("rows", rows_low), ("last", half_low), ("steps", step_sums),
            ("words", jax.ShapeDtypeStruct((nm, own, length, width_own), BFLOAT)),
            ("whole", jax.ShapeDtypeStruct((length, full), FLOAT)), ("rows", sums_type),
        ],
        [row_scratch],
    )
    mixed_own, word_rows = reduction.tie(("down", 0), (mixed_own, word_rows))
    reduction.advance(("down", 0), ("down", 1), ("up", 1))
    mixed_own = reduction.tie(("up", 1), mixed_own)
    up_half = reduction.states["up", 0]
    mixed_own, up_half = lax.optimization_barrier((mixed_own, up_half))
    reduction.states["up", 0] = up_half
    attention_pieces = task_outer(
        place,
        [zero_low, near(zero_low)],
        [mixed_own, near(mixed_other), near(mixed_far)],
        tasks,
        nd,
        early,
        others=[grad_attended, near(grad_attended)],
    )
    reduction.begin("attention", attention_pieces, early)
    kept = reduction.tie(("up", 0), attention_pieces[0][1])
    reduction.states["attention", 0] = (kept, reduction.states["attention", 0][1])
    reduction.advance(("up", 0), ("down", 0), ("down", 1))
    word_rows = reduction.tie(("down", 1), word_rows)
    reduction.advance(("up", 1), ("down", 0), ("down", 1))

    word_rows = lax.all_to_all(word_rows.reshape(nm, tokens, width_own), "mp", 0, 0, tiled=True)
    word_rows = word_rows.reshape(nm * tokens, width_own)
    word_rows = reduction.tie(reduction.last, word_rows)

    def give_back(slot_now, asked_now, sums):
        return match_pairs(word_stored, asked_now, exchange(sums))

    def give_back_round(state):
        turn, given = state
        _, slot_now, wanted_now = distinct(turn, token_flat, rows_owner, nd, slots)
        return turn + 1, given + give_back(
            slot_now, exchange(wanted_now), match_rows(slot_rows, slot_now, word_rows, BFLOAT)
        )

    slot_sums = match_rows(slot_rows, slot, word_rows, BFLOAT)
    slot_sums, table_sums, zero_sums, one_sums, inner_sums, mixed_sums, two_sums = lax.optimization_barrier(
        (slot_sums, table_sums, zero_sums, one_sums, inner_sums, mixed_sums, two_sums)
    )
    slot_sums = reduction.tie(reduction.last, slot_sums)
    word_grad = give_back(slot, asked, slot_sums)
    word_grad = lax.while_loop(lambda state: state[0] < rounds, give_back_round, (jnp.int32(1), word_grad))[1]

    small_rows = length + 2 + vectors.shape[0] + tasks
    rows_part = part_of(small_rows)
    core, x_index = m_index % 2, (m_index // 2) % 2
    collect_place = jnp.concatenate([place_of, task_own, jnp.stack([core])]).astype(jnp.int32)
    keep, send = collect(
        collect_place, table_sums, zero_sums, one_sums, two_sums, inner_sums, mixed_sums, small_rows
    )

    def tied(value):
        return reduction.tie(reduction.last, value)

    came = swap(send, "mp", 1)
    reduction.advance(("attention", 0), ("attention", 1))
    part = jax.ShapeDtypeStruct((rows_part, full), FLOAT)
    keep, send = small_call(add_rows_kernel, x_index, [tied(keep), came], [part, part])
    came = swap(send, "mp", 2)
    reduction.advance(("up", 0), ("up", 1))
    finished = {"down": reduction.complete("down")}
    part = jax.ShapeDtypeStruct((nd // 2, rows_part, slice_width), FLOAT)
    keep, send = small_call(add_columns_kernel, d_index % 2, [tied(keep), came], [part, part])
    came = swap(send, "dp", 1)
    reduction.advance(("attention", 0), ("attention", 1))
    for index, bit in enumerate(z_bits):
        if index == len(z_bits) - 1:
            reduction.advance(("up", 0))
            word_grad = tied(word_grad)
        part = jax.ShapeDtypeStruct((keep.shape[0] // 2, rows_part, slice_width), FLOAT)
        keep, send = small_call(add_blocks_kernel, (d_index // bit) % 2, [tied(keep), came], [part, part])
        came = swap(send, "dp", bit)
    finished["up"] = reduction.complete("up")
    reduction.advance(("attention", 0), ("attention", 1))
    part = jax.ShapeDtypeStruct((rows_part, slice_width), FLOAT)
    (small_grad,) = small_call(add_last_kernel, core, [tied(keep), came], [part])
    came = swap(small_grad, "mp", 2)
    part = jax.ShapeDtypeStruct((2 * rows_part, slice_width), FLOAT)
    (small_grad,) = small_call(join_kernel, x_index, [small_grad, came], [part])
    came = swap(small_grad, "mp", 1)
    part = jax.ShapeDtypeStruct((4 * rows_part, slice_width), FLOAT)
    (small_grad,) = small_call(join_kernel, core, [small_grad, came], [part])
    finished["attention"] = reduction.complete("attention")
    groups, grams = [list(values) for values in zip(*[finished[k] for k in ("attention", "up", "down")])]
    local_squares = jnp.sum(word_grad * word_grad) + jnp.sum(small_grad * small_grad) / nm
    local = jnp.concatenate([jnp.reshape(local_squares, (1,)), local_errors])
    scalars = sum(grams) + jnp.pad(local, (tasks * tasks, LANES - tasks * tasks - local.shape[0]))[None]
    for axis in ("mp", "dp"):
        bit = 1
        while bit < lax.axis_size(axis):
            scalars = scalars + swap(scalars, axis, bit)
            bit *= 2
    *updated, report = update_all(
        task_order, scalars, task_counts, small_grad, word_grad, groups,
        [
            word_table, word_first, word_second, tables, tables_first, tables_second,
            matrices, matrices_first, matrices_second, vectors, vectors_first, vectors_second,
            regressor, regressor_first, regressor_second,
        ],
    )
    return (*updated, report[0, 0], report[0, 1], task_counts)


def solution(mesh):
    placed = (
        P("dp", None),
        P("dp", None),
        P("dp"),
        P(),
        P("dp", None),
        P("dp", None),
        P("dp", "mp"),
        P("dp", "mp"),
        P("dp", "mp"),
        P(None, "dp"),
        P(None, "dp"),
        P(None, "dp"),
        P("dp", "mp"),
        P("dp", "mp"),
        P("dp", "mp"),
        P(None, "dp"),
        P(None, "dp"),
        P(None, "dp"),
        P(None, "dp"),
        P(None, "dp"),
        P(None, "dp"),
    )
    return jax.shard_map(
        on_device,
        mesh=mesh,
        in_specs=placed,
        out_specs=(
            P("dp", "mp"),
            P("dp", "mp"),
            P("dp", "mp"),
            P("dp", "mp"),
            P(None, "dp"),
            P(None, "dp"),
            P(None, "dp"),
            P(None, "dp"),
            P("dp", "mp"),
            P("dp", "mp"),
            P("dp", "mp"),
            P("dp", "mp"),
            P(None, "dp"),
            P(None, "dp"),
            P(None, "dp"),
            P(None, "dp"),
            P(None, "dp"),
            P(None, "dp"),
            P(None, "dp"),
            P(None, "dp"),
            P(),
            P(),
            P(),
        ),
        check_vma=False,
    )
```
